32 devices in a mesh: groups: 2 (over x), node: 2 (over core), local: 8 (over z, y).
Axes of the slice: x: 2, y: 2, z: 4, core: 2. Of those that a mesh axis runs over, the one named last changes fastest.
Arguments:
- tokens: bfloat16 [512, 7168], P(('groups', 'node', 'local')), parts along dimension 0, may hold values from -6 to 6
- expert_ids: int32 [512, 4], P(('groups', 'node', 'local')), parts along dimension 0, may hold values from 0 to 7, all different within a row; in each aligned block of 16 rows (0 to 15, 16 to 31, ...) at most 12 rows name the same one
- gate_weight: bfloat16 [512, 4], P(('groups', 'node', 'local')), parts along dimension 0, may hold values from 0.099609375 to 1
- expert_map: int32 [8], replicated, may hold values from 0 to 7, each once
- w_gate: bfloat16 [16, 7168, 512], P(('node', 'local')), may hold values from -0.0625 to 0.0625
- w_up: bfloat16 [16, 7168, 512], P(('node', 'local')), may hold values from -0.0625 to 0.0625
- w_down: bfloat16 [16, 512, 7168], P(('node', 'local')), may hold values from -0.1875 to 0.1875
Outputs:
- moe_out: bfloat16 [512, 7168], P(('groups', 'node', 'local')), parts along dimension 0
The draws below stay inside these ranges and needn't reach their ends.
There are 2 independent parts, one for each index of `groups`. The reference program is written for one: setup_inputs(seed, part) draws one part's arguments, and reference() takes and returns one part's arrays. A program takes and returns all parts, laid end to end along the dimension named above; an argument that names none is the same for every part. Nothing has to cross between parts.
Inputs may be any that keep to these rules, and one draw needn't show every extreme that they name: `expert_ids`: each row names 4 different experts; among the rows of one device no expert is named by more than 12 rows, a bound that some block reaches. `expert_map`: each slot holds exactly one expert; slot s is shards 2 s and 2 s + 1, on the devices with those indices along node+local.
All inputs are finite; a program needn't handle non-finite values.
Results may differ from the reference program's by a relative error of at most 0.0085.
Values may be sent and summed in bfloat16 or wider, within the bound.
A program may use at most 128 MiB of HBM per device.

```python
import math
import jax
import jax.numpy as jnp
import numpy as np
from jax import lax

D = 7168
FF = 1024
TOK_DEV = 16
HID = 512
EXPERTS = 8
SHARDS = 16
TOPK = 4
MOST = 12
TOKENS = 256


def level_of(stream_key, extent, pieces, least, largest):
    gain, own = 1.0, jax.random.fold_in(stream_key, 6)
    for dim, blocks in pieces:
        draws = jnp.exp(jax.random.uniform(jax.random.fold_in(own, dim), (blocks,), jnp.float32, least / len(pieces), largest / len(pieces)))
        gain = gain * jnp.repeat(draws, extent[dim] // blocks).reshape([-1 if axis == dim else 1 for axis in range(len(extent))])
    return gain


def routed_block(own_key, own, number, rows, count, top, most, lean):
    sequence = jax.random.permutation(own_key, count)
    crowded, common = load_shares(count, rows * top, most, lean, True), load_shares(count, rows * top, most, lean, False)
    places = jnp.arange(count)

    def named(sizes, turn):
        used = int((sizes > 0).sum())
        fixed = max(1, used // 4)
        shifted = fixed + (places - fixed + turn * (used - fixed)) % max(1, count - fixed)
        return jnp.zeros((count,), jnp.int32).at[sequence[jnp.where(places < fixed, places, shifted)]].set(jnp.asarray(sizes, jnp.int32))

    sizes = jnp.where(number % 4 == 0, named(crowded, number // 4), named(common, number - number // 4 - 1))
    mixed = jax.random.permutation(jax.random.fold_in(own, 3), count)
    donor, receiver = mixed[0:count // 2 * 2:2], mixed[1:count // 2 * 2:2]
    slack = jnp.minimum(sizes[donor] - 1, most - sizes[receiver]) // 2
    slack = jnp.where((donor == sequence[0]) | (receiver == sequence[0]) | (sizes[receiver] == 0), 0, jnp.maximum(slack, 0))
    shifted = jax.random.randint(jax.random.fold_in(own, 4), (count // 2,), 0, 1 << 20) % (slack + 1)
    sizes = sizes.at[donor].add(-shifted).at[receiver].add(shifted)
    labels = jnp.searchsorted(jnp.cumsum(sizes), jnp.arange(rows * top), side="right").astype(jnp.int32)
    table = labels.reshape(top, rows).T
    table = table[jax.random.permutation(jax.random.fold_in(own, 1), rows)]
    turn = jax.random.randint(jax.random.fold_in(own, 2), (rows, 1), 0, top)
    return jnp.take_along_axis(table, (jnp.arange(top)[None, :] + turn) % top, axis=1)


def load_shares(amount, total, reach, lean, full):
    weights = [(1 << 20) // math.isqrt(standing ** lean) + 1 for standing in range(1, amount + 1)]
    largest = reach if full else min(reach, max(-(-total // amount), total * weights[0] // sum(weights)))
    least = 1 if total - largest >= amount - 1 else 0
    holding, surplus = [largest] + [least] * (amount - 1), total - largest - least * (amount - 1)
    while surplus > 0:
        movable = [i for i in range(1, amount) if holding[i] < largest] or [i for i in range(1, amount) if holding[i] < reach]
        whole, budget = sum([weights[i] for i in movable]), surplus
        for i in movable:
            extra = min(reach - holding[i], max(1, budget * weights[i] // whole), surplus)
            holding[i] = holding[i] + extra
            surplus = surplus - extra
    return np.array(holding)


def bell_draw(own_key, extent, scale, limit, cuts=(), kind=jnp.bfloat16):
    result = scale * jax.random.normal(own_key, extent, jnp.float32)
    if cuts:
        result = result * level_of(own_key, extent, cuts, -0.22, 0.18)
    return jnp.clip(result, -limit, limit).astype(kind)


def setup_inputs(seed: int = 0, part: int = 0) -> dict:
    key_of = jax.random.split(jax.random.key(seed), 8)
    part_keys = jax.random.split(jax.random.fold_in(key_of[7], part), 8)
    tokens = bell_draw(part_keys[0], (TOKENS, D), 1.0, 6.0, ((0, 16),))
    expert_ids_keys = jax.random.split(jax.random.fold_in(part_keys[1], 1), TOKENS // TOK_DEV)
    expert_ids_turns = jax.random.permutation(jax.random.fold_in(part_keys[1], 3), TOKENS // TOK_DEV)
    expert_ids = jax.vmap(lambda own, number: routed_block(jax.random.fold_in(part_keys[1], 2), own, number, TOK_DEV, EXPERTS, TOPK, MOST, 2))(expert_ids_keys, expert_ids_turns).reshape((TOKENS, TOPK))
    gate_weight = jnp.clip(jnp.exp(math.log(1.0) - 2.306499 * jax.random.uniform(part_keys[2], (TOKENS, TOPK), jnp.float32) ** level_of(part_keys[2], (TOKENS, TOPK), ((0, 16),), -0.2, 0.2)), 0.099609375, 1.0).astype(jnp.bfloat16)
    expert_map = jax.random.permutation(key_of[3], EXPERTS).astype(jnp.int32)
    w_gate = bell_draw(key_of[4], (SHARDS, D, HID), D ** -0.5, 0.0625, ((0, 16),))
    w_up = bell_draw(key_of[5], (SHARDS, D, HID), D ** -0.5, 0.0625, ((0, 16),))
    w_down = bell_draw(key_of[6], (SHARDS, HID, D), FF ** -0.5, 0.1875, ((0, 16),))
    return {"tokens": tokens, "expert_ids": expert_ids, "gate_weight": gate_weight, "expert_map": expert_map, "w_gate": w_gate, "w_up": w_up, "w_down": w_down}


def reference(tokens, expert_ids, gate_weight, expert_map, w_gate, w_up, w_down):
    matches = expert_ids[:, :, None] == jnp.arange(EXPERTS, dtype=jnp.int32)[None, None, :]
    slot_ids = jnp.sum(jnp.where(matches, expert_map[None, None, :], 0), axis=2).astype(jnp.int32)
    gate_values = gate_weight.astype(jnp.float32)

    def shard_term(running, shard_index):
        slot_here = shard_index // 2
        coef = jnp.sum(jnp.where(slot_ids == slot_here, gate_values, 0.0), axis=1)
        gate_proj = jnp.dot(tokens, w_gate[shard_index], preferred_element_type=jnp.float32)
        up_proj = jnp.dot(tokens, w_up[shard_index], preferred_element_type=jnp.float32)
        hidden = (jax.nn.silu(gate_proj) * up_proj).astype(jnp.bfloat16)
        down_proj = jnp.dot(hidden, w_down[shard_index], preferred_element_type=jnp.float32)
        partial_out = (coef[:, None] * down_proj).astype(jnp.bfloat16)
        return running + partial_out.astype(jnp.float32), None

    start = jnp.zeros((TOKENS, D), jnp.float32)
    running, _ = lax.scan(shard_term, start, jnp.arange(SHARDS, dtype=jnp.int32))
    return running.astype(jnp.bfloat16)
```

```python
import functools

import jax
import jax.numpy as jnp
from jax import lax
from jax.experimental import pallas as pl
from jax.experimental.pallas import tpu as pltpu
from jax.sharding import PartitionSpec as P

LANES = 128
GROUP = 2
PARTS_W = 4


def ring_kernel(
    n, ids_ref, gates_ref, map_ref, tokens_ref, wg_hbm, wu_hbm, wd_hbm, out_ref,
    xg, part, insib, rsin, wg, wu, wd,
    tok_sem, w_sem, ag_send, ag_recv, sx_send, sx_recv, sp_send, sp_recv, rs_send, rs_recv,
):
    rows, width = out_ref.shape
    hid = wg.shape[1]
    half = width // LANES // 2 * LANES
    x_cols = ((0, half), (half, width + LANES - half))
    y_cols = ((0, half), (half, width - half))
    pieces = len(x_cols)

    node = lax.axis_index("node")
    local = lax.axis_index("local")
    row_z, row_y = local // 2, local % 2
    pos = row_z * (1 - row_y) + (n - 1 - row_z) * row_y
    step = 1 - 2 * node

    def at(place):
        place = (place + n) % n
        late = place // (n // 2)
        return 2 * place * (1 - late) + (2 * (n - 1 - place) + 1) * late

    ahead = {"local": at(pos + step)}
    behind = {"local": at(pos - step)}
    sibling = {"node": 1 - node}

    tok_copy = pltpu.make_async_copy(tokens_ref, xg.at[pl.ds(0, rows), pl.ds(0, width)], tok_sem)
    tok_copy.start()
    w_copies = []
    for m, (src, dst) in enumerate(((wg_hbm, wg), (wu_hbm, wu), (wd_hbm, wd))):
        span = dst.shape[0] // PARTS_W
        copies = []
        for q in range(PARTS_W):
            block = pl.ds(q * span, span)
            copies.append(pltpu.make_async_copy(src.at[0, block], dst.at[block], w_sem.at[m, q]))
        w_copies.append(copies)
    for q in range(PARTS_W):
        w_copies[0][q].start()
        w_copies[1][q].start()
    for q in range(PARTS_W):
        w_copies[2][q].start()

    lane = lax.broadcasted_iota(jnp.int32, (rows, LANES), 1)
    weights = jnp.zeros((rows, LANES), jnp.float32)
    for k in range(ids_ref.shape[1]):
        weights += jnp.where(ids_ref[:, k:k + 1] == lane, gates_ref[:, k:k + 1].astype(jnp.float32), 0.0)
    xg[0:rows, width:width + LANES] = weights.astype(xg.dtype)

    lane_row = lax.broadcasted_iota(jnp.int32, (1, LANES), 1)
    slots = jnp.full((1, LANES), -1, jnp.int32)
    for e in range(map_ref.shape[0]):
        slots = jnp.where(lane_row == e, map_ref[e], slots)
    chosen = (slots == (node * n + local) // 2).astype(jnp.float32)

    barrier = pltpu.get_barrier_semaphore()
    for device in (ahead, behind, sibling):
        pl.semaphore_signal(barrier, inc=1, device_id=device, device_id_type=pl.DeviceIdType.MESH)
    pl.semaphore_wait(barrier, 3)
    tok_copy.wait()

    def remote(src, dst, send, recv, device):
        return pltpu.make_async_remote_copy(
            src_ref=src, dst_ref=dst, send_sem=send, recv_sem=recv,
            device_id=device, device_id_type=pl.DeviceIdType.MESH,
        )

    def x_block(s, who, h):
        return xg.at[pl.ds((2 * s + who) * rows, rows), pl.ds(*x_cols[h])]

    def gather_copy(s, h):
        return remote(x_block(s - 1, 0, h), x_block(s, 0, h), ag_send.at[s, h], ag_recv.at[s, h], ahead)

    def mirror_copy(s, h):
        return remote(x_block(s, 0, h), x_block(s, 1, h), sx_send.at[s, h], sx_recv.at[s, h], sibling)

    def give_copy(s, h):
        cols = pl.ds(*y_cols[h])
        return remote(
            part.at[pl.ds((2 * s + 1) * rows, rows), cols], insib.at[pl.ds(s * rows, rows), cols],
            sp_send.at[s, h], sp_recv.at[s, h], sibling,
        )

    def sum_copy(s, h):
        cols = pl.ds(*y_cols[h])
        return remote(
            part.at[pl.ds(2 * s * rows, rows), cols], rsin.at[pl.ds(s * rows, rows), cols],
            rs_send.at[s, h], rs_recv.at[s, h], ahead,
        )

    def gather(s):
        for h in range(pieces):
            if s > 0:
                gather_copy(s, h).wait_recv()
            if s < n - 1:
                gather_copy(s + 1, h).start()
            mirror_copy(s, h).start()

    group_rows = GROUP * 2 * rows
    k_tile = width // 4
    n_tile = width // 14

    def hidden_of(g):
        for s in range(g * GROUP, g * GROUP + GROUP):
            for h in range(pieces):
                mirror_copy(s, h).wait_recv()
        if g == 0:
            for copy in w_copies[0] + w_copies[1]:
                copy.wait()
        first = g * group_rows

        def add(k, sums):
            span = pl.ds(pl.multiple_of(k * k_tile, k_tile), k_tile)
            x = xg[pl.ds(first, group_rows), span]
            return (
                sums[0] + jnp.dot(x, wg[span, :], preferred_element_type=jnp.float32),
                sums[1] + jnp.dot(x, wu[span, :], preferred_element_type=jnp.float32),
            )

        zero = jnp.zeros((group_rows, hid), jnp.float32)
        gate, up = lax.fori_loop(0, width // k_tile, add, (zero, zero))
        return (gate / (1.0 + jnp.exp(-gate)) * up).astype(jnp.bfloat16)

    def down(g, hidden):
        if g == 0:
            for copy in w_copies[2]:
                copy.wait()
        first = g * group_rows
        coef = jnp.sum(
            xg[pl.ds(first, group_rows), pl.ds(width, LANES)].astype(jnp.float32) * chosen, axis=1, keepdims=True
        )

        def tile(j, carry):
            span = pl.ds(pl.multiple_of(j * n_tile, n_tile), n_tile)
            y = jnp.dot(hidden, wd[:, span], preferred_element_type=jnp.float32)
            part[pl.ds(first, group_rows), span] = (y * coef).astype(part.dtype)
            return carry

        for h in range(pieces):
            lax.fori_loop(h * 14 // pieces, (h + 1) * 14 // pieces, tile, 0)
            for s in range(g * GROUP, g * GROUP + GROUP):
                give_copy(s, h).start()

    def total(s, h):
        cols = pl.ds(*y_cols[h])
        give_copy(s, h).wait_recv()
        value = part[pl.ds(2 * s * rows, rows), cols].astype(jnp.float32)
        value += insib[pl.ds(s * rows, rows), cols].astype(jnp.float32)
        before = n - 1 if s == 0 else s - 1
        if before > 0:
            sum_copy(before, h).wait_recv()
            value += rsin[pl.ds(before * rows, rows), cols].astype(jnp.float32)
        return value

    def reduce(s):
        for h in range(pieces):
            part[pl.ds(2 * s * rows, rows), pl.ds(*y_cols[h])] = total(s, h).astype(part.dtype)
            sum_copy(s, h).start()

    groups = n // GROUP
    for s in range(3):
        gather(s)
    for g in range(groups):
        hidden = hidden_of(g)
        if g > 0:
            for s in range((g - 1) * GROUP, g * GROUP):
                if s > 0:
                    reduce(s)
        if 2 * g + 3 < n:
            gather(2 * g + 3)
        down(g, hidden)
        if 2 * g + 4 < n:
            gather(2 * g + 4)
    for s in range((groups - 1) * GROUP, n):
        reduce(s)
    for h in range(pieces):
        out_ref[:, y_cols[h][0]:y_cols[h][0] + y_cols[h][1]] = total(0, h).astype(out_ref.dtype)

    for s in range(n):
        for h in range(pieces):
            mirror_copy(s, h).wait_send()
            give_copy(s, h).wait_send()
            if s > 0:
                gather_copy(s, h).wait_send()
                sum_copy(s, h).wait_send()


def body(n, tokens, expert_ids, gate_weight, expert_map, w_gate, w_up, w_down):
    rows, width = tokens.shape
    hid = w_gate.shape[2]
    any_spec = pl.BlockSpec(memory_space=pl.ANY)
    vmem_spec = pl.BlockSpec(memory_space=pltpu.VMEM)
    dma = pltpu.SemaphoreType.DMA
    bf16 = jnp.bfloat16
    flops = 2 * 2 * n * rows * width * hid * 3
    moved = 3 * width * hid * 2
    return pl.pallas_call(
        functools.partial(ring_kernel, n),
        out_shape=jax.ShapeDtypeStruct((rows, width), bf16),
        in_specs=[vmem_spec, vmem_spec, pl.BlockSpec(memory_space=pltpu.SMEM)] + [any_spec] * 4,
        out_specs=vmem_spec,
        scratch_shapes=[
            pltpu.VMEM((2 * n * rows, width + LANES), bf16),
            pltpu.VMEM((2 * n * rows, width), bf16),
            pltpu.VMEM((n * rows, width), bf16),
            pltpu.VMEM((n * rows, width), bf16),
            pltpu.VMEM((width, hid), bf16),
            pltpu.VMEM((width, hid), bf16),
            pltpu.VMEM((hid, width), bf16),
            dma,
            dma((3, PARTS_W)),
        ] + [dma((n, 2))] * 8,
        compiler_params=pltpu.CompilerParams(
            collective_id=0, has_side_effects=True, vmem_limit_bytes=58 * 1024 * 1024
        ),
        cost_estimate=pl.CostEstimate(flops=flops, bytes_accessed=moved, transcendentals=2 * n * rows * hid),
    )(expert_ids, gate_weight, expert_map, tokens, w_gate, w_up, w_down)


def solution(mesh):
    return jax.shard_map(
        functools.partial(body, mesh.shape["local"]),
        mesh=mesh,
        in_specs=(
            P(("groups", "node", "local"), None),
            P(("groups", "node", "local"), None),
            P(("groups", "node", "local"), None),
            P(),
            P(("node", "local"), None, None),
            P(("node", "local"), None, None),
            P(("node", "local"), None, None),
        ),
        out_specs=P(("groups", "node", "local"), None),
        check_vma=False,
    )
```

```python
import functools

import jax
import jax.numpy as jnp
from jax import lax
from jax.experimental import pallas as pl
from jax.experimental.pallas import tpu as pltpu
from jax.sharding import PartitionSpec as P

LANES = 128
GROUP = 2
PIECES = 4
PARTS_W = 4


def ring_kernel(
    n, ids_ref, gates_ref, map_ref, tokens_ref, wg_hbm, wu_hbm, wd_hbm, out_ref,
    xg, part, insib, rsin, wg, wu, wd,
    tok_sem, w_sem, ag_send, ag_recv, sx_send, sx_recv, sp_send, sp_recv, rs_send, rs_recv,
):
    rows, width = out_ref.shape
    hid = wg.shape[1]
    pieces = PIECES
    span_w = width // pieces
    y_cols = [(h * span_w, span_w) for h in range(pieces)]
    x_cols = y_cols[:-1] + [(width - span_w, span_w + LANES)]

    node = lax.axis_index("node")
    local = lax.axis_index("local")
    row_z, row_y = local // 2, local % 2
    pos = row_z * (1 - row_y) + (n - 1 - row_z) * row_y
    step = 1 - 2 * node

    def at(place):
        place = (place + n) % n
        late = place // (n // 2)
        return 2 * place * (1 - late) + (2 * (n - 1 - place) + 1) * late

    ahead = {"local": at(pos + step)}
    behind = {"local": at(pos - step)}
    sibling = {"node": 1 - node}

    tok_copy = pltpu.make_async_copy(tokens_ref, xg.at[pl.ds((2 * n - 2) * rows, rows), pl.ds(0, width)], tok_sem)
    tok_copy.start()
    w_copies = []
    for m, (src, dst) in enumerate(((wg_hbm, wg), (wu_hbm, wu), (wd_hbm, wd))):
        span = dst.shape[0] // PARTS_W
        copies = []
        for q in range(PARTS_W):
            block = pl.ds(q * span, span)
            copies.append(pltpu.make_async_copy(src.at[0, block], dst.at[block], w_sem.at[m, q]))
        w_copies.append(copies)
    for q in range(PARTS_W):
        w_copies[0][q].start()
        w_copies[1][q].start()
    for q in range(PARTS_W):
        w_copies[2][q].start()

    expert = lax.broadcasted_iota(jnp.int32, (LANES, rows), 0)
    weights = jnp.zeros((LANES, rows), jnp.float32)
    for k in range(ids_ref.shape[0]):
        weights += jnp.where(ids_ref[k:k + 1, :] == expert, gates_ref[k:k + 1, :].astype(jnp.float32), 0.0)
    same = lax.broadcasted_iota(jnp.int32, (rows, rows), 0) == lax.broadcasted_iota(jnp.int32, (rows, rows), 1)
    weights = lax.dot_general(
        same.astype(jnp.float32).astype(jnp.bfloat16), weights.astype(jnp.bfloat16), (((1,), (1,)), ((), ())),
        preferred_element_type=jnp.float32,
    )
    xg[(2 * n - 2) * rows:(2 * n - 1) * rows, width:width + LANES] = weights.astype(xg.dtype)

    lane_row = lax.broadcasted_iota(jnp.int32, (1, LANES), 1)
    slots = jnp.full((1, LANES), -1, jnp.int32)
    for e in range(map_ref.shape[0]):
        slots = jnp.where(lane_row == e, map_ref[e], slots)
    chosen = (slots == (node * n + local) // 2).astype(jnp.float32)

    barrier = pltpu.get_barrier_semaphore()
    for device in (ahead, behind, sibling):
        pl.semaphore_signal(barrier, inc=1, device_id=device, device_id_type=pl.DeviceIdType.MESH)
    pl.semaphore_wait(barrier, 3)
    tok_copy.wait()

    def remote(src, dst, send, recv, device):
        return pltpu.make_async_remote_copy(
            src_ref=src, dst_ref=dst, send_sem=send, recv_sem=recv,
            device_id=device, device_id_type=pl.DeviceIdType.MESH,
        )

    def slot(s, who):
        return pl.ds((2 * ((s - 1) % n) + who) * rows, rows)

    def x_block(s, who, h):
        return xg.at[slot(s, who), pl.ds(*x_cols[h])]

    def gather_copy(s, h):
        return remote(x_block(s - 1, 0, h), x_block(s, 0, h), ag_send.at[s, h], ag_recv.at[s, h], ahead)

    def mirror_copy(s, h):
        return remote(x_block(s, 0, h), x_block(s, 1, h), sx_send.at[s, h], sx_recv.at[s, h], sibling)

    def give_copy(s, h):
        cols = pl.ds(*y_cols[h])
        return remote(
            part.at[slot(s, 1), cols], insib.at[pl.ds(s * rows, rows), cols],
            sp_send.at[s, h], sp_recv.at[s, h], sibling,
        )

    def sum_copy(s, h):
        cols = pl.ds(*y_cols[h])
        return remote(
            part.at[slot(s, 0), cols], rsin.at[pl.ds(s * rows, rows), cols],
            rs_send.at[s, h], rs_recv.at[s, h], ahead,
        )

    def gather(s, h):
        if s > 0:
            gather_copy(s, h).wait_recv()
        if s < n - 1:
            gather_copy(s + 1, h).start()
        mirror_copy(s, h).start()

    group_rows = GROUP * 2 * rows
    k_tile = width // PIECES
    n_tile = width // PIECES

    def chunks_of(g):
        return [s % n for s in range(g * GROUP + 1, g * GROUP + GROUP + 1)]

    def hidden_of(g, between):
        for s in chunks_of(g):
            for h in range(pieces):
                mirror_copy(s, h).wait_recv()
        first = g * group_rows
        gate = jnp.zeros((group_rows, hid), jnp.float32)
        up = jnp.zeros((group_rows, hid), jnp.float32)
        for k in range(pieces):
            if g == 0:
                w_copies[0][k].wait()
                w_copies[1][k].wait()
            span = pl.ds(k * k_tile, k_tile)
            x = xg[pl.ds(first, group_rows), span]
            gate += jnp.dot(x, wg[span, :], preferred_element_type=jnp.float32)
            up += jnp.dot(x, wu[span, :], preferred_element_type=jnp.float32)
            between(k)
        return (gate / (1.0 + jnp.exp(-gate)) * up).astype(jnp.bfloat16)

    def down(g, hidden, between):
        if g == 0:
            for copy in w_copies[2]:
                copy.wait()
        first = g * group_rows
        coef = jnp.sum(
            xg[pl.ds(first, group_rows), pl.ds(width, LANES)].astype(jnp.float32) * chosen, axis=1, keepdims=True
        )
        for h in range(pieces):
            span = pl.ds(h * n_tile, n_tile)
            y = jnp.dot(hidden, wd[:, span], preferred_element_type=jnp.float32)
            part[pl.ds(first, group_rows), span] = (y * coef).astype(part.dtype)
            for s in chunks_of(g):
                give_copy(s, h).start()
            between(h)

    def total(s, h):
        cols = pl.ds(*y_cols[h])
        give_copy(s, h).wait_recv()
        value = part[slot(s, 0), cols].astype(jnp.float32)
        value += insib[pl.ds(s * rows, rows), cols].astype(jnp.float32)
        before = n - 1 if s == 0 else s - 1
        if before > 0:
            sum_copy(before, h).wait_recv()
            value += rsin[pl.ds(before * rows, rows), cols].astype(jnp.float32)
        return value

    def reduce(s, h):
        part[slot(s, 0), pl.ds(*y_cols[h])] = total(s, h).astype(part.dtype)
        sum_copy(s, h).start()

    for h in range(pieces):
        gather(0, h)
    for s in (1, 2):
        for h in range(pieces):
            gather(s, h)

    def between(gather_step, reduce_step):
        def run(h):
            if gather_step < n:
                gather(gather_step, h)
            if 0 < reduce_step < n:
                reduce(reduce_step, h)
        return run

    groups = n // GROUP
    for g in range(groups):
        hidden = hidden_of(g, between(2 * g + 3, 2 * g - 1))
        down(g, hidden, between(2 * g + 4, 2 * g))
    for h in range(pieces):
        reduce(n - 1, h)
    for h in range(pieces):
        out_ref[:, y_cols[h][0]:y_cols[h][0] + y_cols[h][1]] = total(0, h).astype(out_ref.dtype)

    for s in range(n):
        for h in range(pieces):
            mirror_copy(s, h).wait_send()
            give_copy(s, h).wait_send()
            if s > 0:
                gather_copy(s, h).wait_send()
                sum_copy(s, h).wait_send()


def body(n, tokens, expert_ids, gate_weight, expert_map, w_gate, w_up, w_down):
    rows, width = tokens.shape
    hid = w_gate.shape[2]
    any_spec = pl.BlockSpec(memory_space=pl.ANY)
    vmem_spec = pl.BlockSpec(memory_space=pltpu.VMEM)
    dma = pltpu.SemaphoreType.DMA
    bf16 = jnp.bfloat16
    flops = 2 * 2 * n * rows * width * hid * 3
    moved = 3 * width * hid * 2
    return pl.pallas_call(
        functools.partial(ring_kernel, n),
        out_shape=jax.ShapeDtypeStruct((rows, width), bf16),
        in_specs=[vmem_spec, vmem_spec, pl.BlockSpec(memory_space=pltpu.SMEM)] + [any_spec] * 4,
        out_specs=vmem_spec,
        scratch_shapes=[
            pltpu.VMEM((2 * n * rows, width + LANES), bf16),
            pltpu.VMEM((2 * n * rows, width), bf16),
            pltpu.VMEM((n * rows, width), bf16),
            pltpu.VMEM((n * rows, width), bf16),
            pltpu.VMEM((width, hid), bf16),
            pltpu.VMEM((width, hid), bf16),
            pltpu.VMEM((hid, width), bf16),
            dma,
            dma((3, PARTS_W)),
        ] + [dma((n, PIECES))] * 8,
        compiler_params=pltpu.CompilerParams(
            collective_id=0, has_side_effects=True, vmem_limit_bytes=58 * 1024 * 1024
        ),
        cost_estimate=pl.CostEstimate(flops=flops, bytes_accessed=moved, transcendentals=2 * n * rows * hid),
    )(expert_ids.T, gate_weight.T, expert_map, tokens, w_gate, w_up, w_down)


def solution(mesh):
    return jax.shard_map(
        functools.partial(body, mesh.shape["local"]),
        mesh=mesh,
        in_specs=(
            P(("groups", "node", "local"), None),
            P(("groups", "node", "local"), None),
            P(("groups", "node", "local"), None),
            P(),
            P(("node", "local"), None, None),
            P(("node", "local"), None, None),
            P(("node", "local"), None, None),
        ),
        out_specs=P(("groups", "node", "local"), None),
        check_vma=False,
    )
```

```python
import functools

import jax
import jax.numpy as jnp
from jax import lax
from jax.experimental import pallas as pl
from jax.experimental.pallas import tpu as pltpu
from jax.sharding import PartitionSpec as P

LANES = 128
GROUP = 2
PIECES = 4
PARTS_W = 4


def ring_kernel(
    n, ids_ref, gates_ref, map_ref, tokens_ref, wg_hbm, wu_hbm, wd_hbm, out_ref,
    xg, part, insib, rsin, wg, wu, wd,
    tok_sem, w_sem, ag_send, ag_recv, sx_send, sx_recv, sp_send, sp_recv, rs_send, rs_recv,
):
    rows, width = out_ref.shape
    hid = wg.shape[1]
    pieces = PIECES
    span_w = width // pieces
    y_cols = [(h * span_w, span_w) for h in range(pieces)]
    x_cols = y_cols[:-1] + [(width - span_w, span_w + LANES)]

    node = lax.axis_index("node")
    local = lax.axis_index("local")
    row_z, row_y = local // 2, local % 2
    pos = row_z * (1 - row_y) + (n - 1 - row_z) * row_y
    step = 1 - 2 * node

    def at(place):
        place = (place + n) % n
        late = place // (n // 2)
        return 2 * place * (1 - late) + (2 * (n - 1 - place) + 1) * late

    ahead = {"local": at(pos + step)}
    behind = {"local": at(pos - step)}
    sibling = {"node": 1 - node}

    tok_copy = pltpu.make_async_copy(tokens_ref, xg.at[pl.ds((2 * n - 2) * rows, rows), pl.ds(0, width)], tok_sem)
    tok_copy.start()
    w_copies = []
    for m, (src, dst) in enumerate(((wg_hbm, wg), (wu_hbm, wu), (wd_hbm, wd))):
        span = dst.shape[0] // PARTS_W
        copies = []
        for q in range(PARTS_W):
            block = pl.ds(q * span, span)
            copies.append(pltpu.make_async_copy(src.at[0, block], dst.at[block], w_sem.at[m, q]))
        w_copies.append(copies)
    for q in range(PARTS_W):
        w_copies[0][q].start()
        w_copies[1][q].start()
    for q in range(PARTS_W):
        w_copies[2][q].start()

    expert = lax.broadcasted_iota(jnp.int32, (LANES, rows), 0)
    weights = jnp.zeros((LANES, rows), jnp.float32)
    for k in range(ids_ref.shape[0]):
        weights += jnp.where(ids_ref[k:k + 1, :] == expert, gates_ref[k:k + 1, :].astype(jnp.float32), 0.0)
    same = lax.broadcasted_iota(jnp.int32, (rows, rows), 0) == lax.broadcasted_iota(jnp.int32, (rows, rows), 1)
    weights = lax.dot_general(
        same.astype(jnp.float32).astype(jnp.bfloat16), weights.astype(jnp.bfloat16), (((1,), (1,)), ((), ())),
        preferred_element_type=jnp.float32,
    )
    xg[(2 * n - 2) * rows:(2 * n - 1) * rows, width:width + LANES] = weights.astype(xg.dtype)

    lane_row = lax.broadcasted_iota(jnp.int32, (1, LANES), 1)
    slots = jnp.full((1, LANES), -1, jnp.int32)
    for e in range(map_ref.shape[0]):
        slots = jnp.where(lane_row == e, map_ref[e], slots)
    chosen = (slots == (node * n + local) // 2).astype(jnp.float32)

    barrier = pltpu.get_barrier_semaphore()
    for device in (ahead, behind, sibling):
        pl.semaphore_signal(barrier, inc=1, device_id=device, device_id_type=pl.DeviceIdType.MESH)
    pl.semaphore_wait(barrier, 3)
    tok_copy.wait()

    def remote(src, dst, send, recv, device):
        return pltpu.make_async_remote_copy(
            src_ref=src, dst_ref=dst, send_sem=send, recv_sem=recv,
            device_id=device, device_id_type=pl.DeviceIdType.MESH,
        )

    def slot(s, who):
        return pl.ds((2 * ((s - 1) % n) + who) * rows, rows)

    def x_block(s, who, h):
        return xg.at[slot(s, who), pl.ds(*x_cols[h])]

    def gather_copy(s, h):
        return remote(x_block(s - 1, 0, h), x_block(s, 0, h), ag_send.at[s, h], ag_recv.at[s, h], ahead)

    def mirror_copy(s, h):
        return remote(x_block(s, 0, h), x_block(s, 1, h), sx_send.at[s, h], sx_recv.at[s, h], sibling)

    def give_copy(s, h):
        cols = pl.ds(*y_cols[h])
        return remote(
            part.at[slot(s, 1), cols], insib.at[pl.ds(s * rows, rows), cols],
            sp_send.at[s, h], sp_recv.at[s, h], sibling,
        )

    def sum_copy(s, h):
        cols = pl.ds(*y_cols[h])
        return remote(
            part.at[slot(s, 0), cols], rsin.at[pl.ds(s * rows, rows), cols],
            rs_send.at[s, h], rs_recv.at[s, h], ahead,
        )

    def gather(s, h):
        if s > 0:
            gather_copy(s, h).wait_recv()
        if s < n - 1:
            gather_copy(s + 1, h).start()
        mirror_copy(s, h).start()

    group_rows = GROUP * 2 * rows
    k_tile = width // PIECES
    n_tile = width // PIECES

    def chunks_of(g):
        return [s % n for s in range(g * GROUP + 1, g * GROUP + GROUP + 1)]

    def hidden_of(g, between):
        for s in chunks_of(g):
            for h in range(pieces):
                mirror_copy(s, h).wait_recv()
        first = g * group_rows
        gate = jnp.zeros((group_rows, hid), jnp.float32)
        up = jnp.zeros((group_rows, hid), jnp.float32)
        for k in range(pieces):
            if g == 0:
                w_copies[0][k].wait()
                w_copies[1][k].wait()
            span = pl.ds(k * k_tile, k_tile)
            x = xg[pl.ds(first, group_rows), span]
            gate += jnp.dot(x, wg[span, :], preferred_element_type=jnp.float32)
            up += jnp.dot(x, wu[span, :], preferred_element_type=jnp.float32)
            between(k)
        return (gate / (1.0 + jnp.exp(-gate)) * up).astype(jnp.bfloat16)

    def down(g, hidden, between):
        if g == 0:
            for copy in w_copies[2]:
                copy.wait()
        first = g * group_rows
        coef = jnp.sum(
            xg[pl.ds(first, group_rows), pl.ds(width, LANES)].astype(jnp.float32) * chosen, axis=1, keepdims=True
        )
        for h in range(pieces):
            span = pl.ds(h * n_tile, n_tile)
            y = jnp.dot(hidden, wd[:, span], preferred_element_type=jnp.float32)
            part[pl.ds(first, group_rows), span] = (y * coef).astype(part.dtype)
            for s in chunks_of(g):
                give_copy(s, h).start()
            between(h)

    def total(s, h):
        cols = pl.ds(*y_cols[h])
        give_copy(s, h).wait_recv()
        value = part[slot(s, 0), cols].astype(jnp.float32)
        value += insib[pl.ds(s * rows, rows), cols].astype(jnp.float32)
        before = n - 1 if s == 0 else s - 1
        if before > 0:
            sum_copy(before, h).wait_recv()
            value += rsin[pl.ds(before * rows, rows), cols].astype(jnp.float32)
        return value

    def reduce(s, h):
        part[slot(s, 0), pl.ds(*y_cols[h])] = total(s, h).astype(part.dtype)
        sum_copy(s, h).start()

    for h in range(pieces):
        gather(0, h)
    for s in (1, 2):
        for h in range(pieces):
            gather(s, h)

    def between(gather_step, reduce_step, lag):
        def run(h):
            if 0 < reduce_step < n and h >= lag:
                reduce(reduce_step, h - lag)
            if gather_step < n:
                gather(gather_step, h)
        return run

    groups = n // GROUP
    for g in range(groups):
        hidden = hidden_of(g, between(2 * g + 3, 2 * g, 0))
        down(g, hidden, between(2 * g + 4, 2 * g + 1, 1))
        reduce(2 * g + 1, pieces - 1)
    for h in range(pieces):
        out_ref[:, y_cols[h][0]:y_cols[h][0] + y_cols[h][1]] = total(0, h).astype(out_ref.dtype)

    for s in range(n):
        for h in range(pieces):
            mirror_copy(s, h).wait_send()
            give_copy(s, h).wait_send()
            if s > 0:
                gather_copy(s, h).wait_send()
                sum_copy(s, h).wait_send()


def body(n, tokens, expert_ids, gate_weight, expert_map, w_gate, w_up, w_down):
    rows, width = tokens.shape
    hid = w_gate.shape[2]
    any_spec = pl.BlockSpec(memory_space=pl.ANY)
    vmem_spec = pl.BlockSpec(memory_space=pltpu.VMEM)
    dma = pltpu.SemaphoreType.DMA
    bf16 = jnp.bfloat16
    flops = 2 * 2 * n * rows * width * hid * 3
    moved = 3 * width * hid * 2
    return pl.pallas_call(
        functools.partial(ring_kernel, n),
        out_shape=jax.ShapeDtypeStruct((rows, width), bf16),
        in_specs=[vmem_spec, vmem_spec, pl.BlockSpec(memory_space=pltpu.SMEM)] + [any_spec] * 4,
        out_specs=vmem_spec,
        scratch_shapes=[
            pltpu.VMEM((2 * n * rows, width + LANES), bf16),
            pltpu.VMEM((2 * n * rows, width), bf16),
            pltpu.VMEM((n * rows, width), bf16),
            pltpu.VMEM((n * rows, width), bf16),
            pltpu.VMEM((width, hid), bf16),
            pltpu.VMEM((width, hid), bf16),
            pltpu.VMEM((hid, width), bf16),
            dma,
            dma((3, PARTS_W)),
        ] + [dma((n, PIECES))] * 8,
        compiler_params=pltpu.CompilerParams(
            collective_id=0, has_side_effects=True, vmem_limit_bytes=58 * 1024 * 1024
        ),
        cost_estimate=pl.CostEstimate(flops=flops, bytes_accessed=moved, transcendentals=2 * n * rows * hid),
    )(expert_ids.T, gate_weight.T, expert_map, tokens, w_gate, w_up, w_down)


def solution(mesh):
    return jax.shard_map(
        functools.partial(body, mesh.shape["local"]),
        mesh=mesh,
        in_specs=(
            P(("groups", "node", "local"), None),
            P(("groups", "node", "local"), None),
            P(("groups", "node", "local"), None),
            P(),
            P(("node", "local"), None, None),
            P(("node", "local"), None, None),
            P(("node", "local"), None, None),
        ),
        out_specs=P(("groups", "node", "local"), None),
        check_vma=False,
    )
```
